256 devices in a mesh: grp: 16 (over x, y_lo, core), seq: 16 (over z, y_hi).
Axes of the slice: x: 4, y: 4 (y_hi: 2, y_lo: 2; y = y_hi * 2 + y_lo), z: 8, core: 2. Of those that a mesh axis runs over, the one named last changes fastest.
Arguments:
- queries: bfloat16 [16, 3072, 2048], P('grp', 'seq'), may hold values from -24 to 24
- template_suffix_keys: bfloat16 [16, 3072, 1024], P('grp', 'seq'), may hold values from -6 to 6
- template_suffix_values: bfloat16 [16, 3072, 1024], P('grp', 'seq'), may hold values from -6 to 6
- cached_prefix_keys: bfloat16 [4096, 1024], P('grp'), may hold values from -9 to 9
- cached_prefix_values: bfloat16 [4096, 1024], P('grp'), may hold values from -6 to 6
- lengths: int32 [16], P('grp'), may hold values from 192 to 3072, as said below
Outputs:
- attended: bfloat16 [16, 3072, 2048], P('grp', 'seq')
The draws below stay inside these ranges and needn't reach their ends.
Inputs may be any that keep to these rules, and one draw needn't show every extreme that they name: `lengths`: some template has length 3072.
All inputs are finite; a program needn't handle non-finite values.
Results may differ from the reference program's by a relative error of at most 0.018.
Values may be sent and summed in bfloat16 or wider, within the bound.
No kernel may reach another device: no remote copies, remote signals or barrier semaphores. Data moves between devices by JAX's collectives and lax.ppermute only.
A program may use at most 256 MiB of HBM per device.

```python
import jax
import jax.numpy as jnp
from jax import lax

HQ = 16
LOCAL_KV_HEADS = 8
HEAD_SIZE = 128
QUERY_PER_KV = 2
ROWS = 192
TEMPLATE_COUNT = 16
SUFFIX_LENGTH = 3072
PREFIX_LENGTH = 4096


def draw_queries(key, part):
    unmasked_scores = jnp.clip(jax.random.normal(jax.random.fold_in(key, 1), (TEMPLATE_COUNT, SUFFIX_LENGTH, HQ * HEAD_SIZE), jnp.float32), -6.0, 6.0)
    return unmasked_scores.astype(jnp.bfloat16)


def draw_cached_prefix_keys(key, part):
    unmasked_scores = jnp.clip(jax.random.normal(jax.random.fold_in(key, 3), (PREFIX_LENGTH, LOCAL_KV_HEADS * HEAD_SIZE), jnp.float32), -6.0, 6.0)
    return unmasked_scores.astype(jnp.bfloat16)


def draw_lengths(key, part):
    spread = SUFFIX_LENGTH - ROWS + 1
    uniform_pick = jax.random.randint(jax.random.fold_in(key, 5), (TEMPLATE_COUNT,), 0, spread)
    result = ROWS + uniform_pick * uniform_pick // spread
    full_index = jax.random.randint(jax.random.fold_in(key, 6), (), 0, TEMPLATE_COUNT)
    return jnp.where(jnp.arange(TEMPLATE_COUNT) == full_index, SUFFIX_LENGTH, result).astype(jnp.int32)


def steps_of(stream_key, dims, pieces, low, high):
    gain, own = 1.0, jax.random.fold_in(stream_key, 6)
    for dim, parts in pieces:
        steps = jnp.exp(jax.random.uniform(jax.random.fold_in(own, dim), (parts,), jnp.float32, low / len(pieces), high / len(pieces)))
        gain = gain * jnp.repeat(steps, dims[dim] // parts).reshape([-1 if axis == dim else 1 for axis in range(len(dims))])
    return gain


def normal_values(stream_key, extent, deviation, bound, pieces=(), held_as=jnp.bfloat16):
    values = jax.random.normal(stream_key, extent, jnp.float32) * deviation
    if len(pieces) > 0:
        values = steps_of(stream_key, extent, pieces, -0.22, 0.18) * values
    return jnp.clip(values, min=-bound, max=bound).astype(held_as)


def setup_inputs(seed: int = 0) -> dict:
    splits = jax.random.split(jax.random.key(seed), 7)
    queries = draw_queries(jax.random.fold_in(splits[6], 71), 0)
    template_suffix_keys = normal_values(splits[1], (TEMPLATE_COUNT, SUFFIX_LENGTH, LOCAL_KV_HEADS * HEAD_SIZE), 1.0, 6.0, ((0, 16), (1, 16)))
    template_suffix_values = normal_values(splits[2], (TEMPLATE_COUNT, SUFFIX_LENGTH, LOCAL_KV_HEADS * HEAD_SIZE), 1.0, 6.0, ((0, 16), (1, 16)))
    cached_prefix_keys = draw_cached_prefix_keys(jax.random.fold_in(splits[6], 71), 0)
    cached_prefix_values = normal_values(splits[4], (PREFIX_LENGTH, LOCAL_KV_HEADS * HEAD_SIZE), 1.0, 6.0, ((0, 16),))
    lengths = draw_lengths(jax.random.fold_in(splits[6], 71), 0)
    return dict(queries=queries, template_suffix_keys=template_suffix_keys, template_suffix_values=template_suffix_values, cached_prefix_keys=cached_prefix_keys, cached_prefix_values=cached_prefix_values, lengths=lengths)


query_scale = 168.0 ** -0.5


def reference(queries, template_suffix_keys, template_suffix_values, cached_prefix_keys, cached_prefix_values, lengths):
    row_ids = jnp.arange(SUFFIX_LENGTH, dtype=jnp.int32)
    col_ids = jnp.arange(PREFIX_LENGTH + SUFFIX_LENGTH, dtype=jnp.int32)
    visible = col_ids[None, :] < PREFIX_LENGTH + row_ids[:, None] + 1

    def one_template(inputs):
        rows_of_queries, rows_of_keys, rows_of_values, suffix_length = inputs
        joined_keys = jnp.concatenate([cached_prefix_keys, rows_of_keys], axis=0).reshape(PREFIX_LENGTH + SUFFIX_LENGTH, LOCAL_KV_HEADS, HEAD_SIZE)
        joined_values = jnp.concatenate([cached_prefix_values, rows_of_values], axis=0).reshape(PREFIX_LENGTH + SUFFIX_LENGTH, LOCAL_KV_HEADS, HEAD_SIZE)
        heads_of_queries = rows_of_queries.reshape(SUFFIX_LENGTH, LOCAL_KV_HEADS, QUERY_PER_KV, HEAD_SIZE)

        def single_head(head):
            query_part = heads_of_queries[:, head].astype(jnp.float32)
            key_part = joined_keys[:, head].astype(jnp.float32)
            value_part = joined_values[:, head].astype(jnp.float32)
            scores = jnp.einsum("rgd,nd->grn", query_part, key_part) * query_scale
            scores = jnp.where(visible[None], scores, jnp.float32(-1e30))
            row_peak = jnp.max(scores, axis=-1, keepdims=True)
            raw = jnp.exp(scores - row_peak)
            row_total = jnp.sum(raw, axis=-1)
            weights = raw.astype(jnp.bfloat16).astype(jnp.float32)
            summed = jnp.einsum("grn,nd->grd", weights, value_part)
            return summed / row_total[..., None]

        each_head_result = lax.map(single_head, jnp.arange(LOCAL_KV_HEADS, dtype=jnp.int32))
        result = jnp.transpose(each_head_result, (2, 0, 1, 3)).reshape(SUFFIX_LENGTH, HQ * HEAD_SIZE)
        live_rows = row_ids < suffix_length
        return jnp.where(live_rows[:, None], result, jnp.float32(0.0)).astype(jnp.bfloat16)

    return lax.map(one_template, (queries, template_suffix_keys, template_suffix_values, lengths))
```

```python
import jax
import jax.numpy as jnp
from jax import lax
from jax.experimental import pallas as pl
from jax.experimental.pallas import tpu as pltpu
from jax.sharding import Mesh, PartitionSpec as P

LOCAL_KV_HEADS = 8
HEAD_SIZE = 128
QUERY_PER_KV = 2
ROWS = 192
BLOCKS = 8
ALL_ROWS = BLOCKS * ROWS
PREFIX_HALF = 2048
ROW_TILE = 384
KEY_TILE = 512

query_scale = 168.0 ** (-0.5)
log2_e = 1.4426950408889634
total_bound = 1e37
hs = HEAD_SIZE
q_lanes = slice(0, 2 * hs)
k_lanes = slice(2 * hs, 3 * hs)
v_lanes = slice(3 * hs, 4 * hs)


def scores_of(query_pair, keys):
    return lax.dot_general(
        query_pair,
        jnp.concatenate([keys, keys], axis=1),
        (((1,), (1,)), ((), ())),
        preferred_element_type=jnp.float32,
    )


def weights_of(scores, shift):
    return jnp.exp2(scores - jnp.concatenate([shift] * (scores.shape[1] // 128), axis=1))


def summed_of(weights, values):
    return lax.dot_general(
        weights.astype(jnp.bfloat16),
        jnp.concatenate([values, jnp.ones_like(values)], axis=1),
        (((1,), (0,)), ((), ())),
        preferred_element_type=jnp.float32,
    )


def pair_of(queries):
    queries = jnp.concatenate([queries[:, 0:hs], queries[:, hs : 2 * hs]], axis=0)
    scaled = queries.astype(jnp.float32) * (query_scale * log2_e)
    high = scaled.astype(jnp.bfloat16)
    low = (scaled - high.astype(jnp.float32)).astype(jnp.bfloat16)
    return jnp.concatenate([high, low], axis=1)


def prefix_kernel(mine, prefix_a, prefix_b, shifts, accum):
    tiles = [(p, i) for p in (prefix_a, prefix_b) for i in range(0, PREFIX_HALF, KEY_TILE)]

    @pl.loop(0, ALL_ROWS // ROW_TILE)
    def _(step):
        rows = pl.ds(pl.multiple_of(step * ROW_TILE, ROW_TILE), ROW_TILE)
        pair = pair_of(mine[rows, q_lanes])
        first = scores_of(pair, prefix_a[0:256, 0:hs])
        shift = jnp.broadcast_to(jnp.max(first, axis=1, keepdims=True), (2 * ROW_TILE, 128))
        scores = scores_of(pair, prefix_a[0:KEY_TILE, 0:hs])
        total = None
        for j, (ref, start) in enumerate(tiles):
            following = None
            if j + 1 < len(tiles):
                next_ref, next_start = tiles[j + 1]
                following = scores_of(pair, next_ref[next_start : next_start + KEY_TILE, 0:hs])
            added = summed_of(weights_of(scores, shift), ref[start : start + KEY_TILE, hs : 2 * hs])
            total = added if total is None else total + added
            scores = following
        for member in range(QUERY_PER_KV):
            part = slice(member * ROW_TILE, (member + 1) * ROW_TILE)
            shifts[member, rows, :] = shift[part]
            accum[member, rows, :] = total[part]


def suffix_kernel(meta, mine, other, shifts, accum, prefix_a, prefix_b, out, peaks, again):
    second = meta[0]
    length = meta[1]
    row_ids = lax.broadcasted_iota(jnp.int32, (2 * ROWS, 2 * ROWS), 0)
    row_ids = jnp.where(row_ids < ROWS, row_ids, row_ids - ROWS)
    col_ids = lax.broadcasted_iota(jnp.int32, (2 * ROWS, 2 * ROWS), 1)
    visible = ((col_ids < ROWS) & (col_ids <= row_ids)) | ((col_ids >= ROWS) & (second == 1))

    def keys_of(block, which):
        parts = []
        if block > 0:
            parts += [mine[0 : block * ROWS, (k_lanes, v_lanes)[which]]]
            parts += [other[0 : block * ROWS, which * hs : (which + 1) * hs]]
        rows = slice(block * ROWS, (block + 1) * ROWS)
        parts += [mine[rows, (k_lanes, v_lanes)[which]]]
        parts += [other[rows, which * hs : (which + 1) * hs]]
        return jnp.concatenate(parts, axis=0)

    def both(ref, block):
        return jnp.concatenate([ref[m, block * ROWS : (block + 1) * ROWS, :] for m in range(2)], axis=0)

    def suffix_scores(block):
        return scores_of(pair_of(mine[block * ROWS : (block + 1) * ROWS, q_lanes]), keys_of(block, 0))

    def finish(block, total):
        result = total[:, 0:hs] / total[:, hs : 2 * hs]
        result = jnp.concatenate([result[0:ROWS], result[ROWS : 2 * ROWS]], axis=1)
        row = lax.broadcasted_iota(jnp.int32, (ROWS, 2 * hs), 0)
        live = (2 * block + second) * ROWS + row < length
        return jnp.where(live, result, 0.0).astype(jnp.bfloat16)

    scores = suffix_scores(0)
    beyond = jnp.zeros((2 * ROWS, hs), jnp.float32)
    for block in range(BLOCKS):
        following = suffix_scores(block + 1) if block + 1 < BLOCKS else None
        weights = weights_of(scores, both(shifts, block))
        edge = 2 * ROWS * block
        masked = jnp.where(visible, weights[:, edge:], 0.0)
        weights = jnp.concatenate([weights[:, :edge], masked], axis=1) if block > 0 else masked
        total = both(accum, block) + summed_of(weights, keys_of(block, 1))
        beyond = jnp.maximum(beyond, jnp.where(total[:, hs:] < total_bound, 0.0, 1.0))
        out[block * ROWS : (block + 1) * ROWS, :] = finish(block, total)
        scores = following

    @pl.when(jnp.max(beyond) > 0.0)
    def _():
        @pl.loop(0, BLOCKS)
        def _(block):
            rows = pl.ds(pl.multiple_of(block * ROWS, ROWS), ROWS)
            pair = pair_of(mine[rows, q_lanes])
            peaks[...] = jnp.full((2 * ROWS, 128), -1e30, jnp.float32)
            again[...] = jnp.zeros((2 * ROWS, 2 * hs), jnp.float32)

            def step(keys, values, seen):
                part = scores_of(pair, keys)
                if seen is not None:
                    part = jnp.where(seen, part, -1e30)
                old = peaks[:, 0:1]
                new = jnp.maximum(old, jnp.max(part, axis=1, keepdims=True))
                weights = jnp.exp2(part - new)
                again[...] = again[...] * jnp.exp2(old - new) + summed_of(weights, values)
                peaks[...] = jnp.broadcast_to(new, (2 * ROWS, 128))

            for ref in (prefix_a, prefix_b):

                @pl.loop(0, PREFIX_HALF // 256)
                def _(i):
                    keys = pl.ds(pl.multiple_of(i * 256, 256), 256)
                    step(ref[keys, 0:hs], ref[keys, hs : 2 * hs], None)

            row = lax.broadcasted_iota(jnp.int32, (2 * ROWS, ROWS), 0)
            row = jnp.where(row < ROWS, row, row - ROWS)
            col = lax.broadcasted_iota(jnp.int32, (2 * ROWS, ROWS), 1)

            @pl.loop(0, block + 1)
            def _(i):
                keys = pl.ds(pl.multiple_of(i * ROWS, ROWS), ROWS)
                step(mine[keys, k_lanes], mine[keys, v_lanes], (col <= row) | (i < block))
                full = (i < block) | (second == 1)
                step(other[keys, 0:hs], other[keys, hs : 2 * hs], (col >= 0) & full)

            out[rows, :] = finish(block, again[...])


in_vmem = pl.BlockSpec(memory_space=pltpu.VMEM)


def prefix_part(mine, prefix_a, prefix_b):
    count = 2 * ALL_ROWS * 2 * PREFIX_HALF
    return pl.pallas_call(
        prefix_kernel,
        out_shape=(
            jax.ShapeDtypeStruct((2, ALL_ROWS, 128), jnp.float32),
            jax.ShapeDtypeStruct((2, ALL_ROWS, 2 * hs), jnp.float32),
        ),
        in_specs=[in_vmem] * 3,
        out_specs=(in_vmem, in_vmem),
        compiler_params=pltpu.CompilerParams(vmem_limit_bytes=24 << 20),
        cost_estimate=pl.CostEstimate(
            flops=count * 256 * 4, bytes_accessed=8 << 20, transcendentals=count
        ),
    )(mine, prefix_a, prefix_b)


def suffix_part(meta, mine, other, shifts, accum, prefix_a, prefix_b):
    count = 2 * ALL_ROWS * ALL_ROWS
    return pl.pallas_call(
        suffix_kernel,
        out_shape=jax.ShapeDtypeStruct((ALL_ROWS, 2 * hs), jnp.bfloat16),
        in_specs=[pl.BlockSpec(memory_space=pltpu.SMEM)] + [in_vmem] * 6,
        out_specs=in_vmem,
        scratch_shapes=[
            pltpu.VMEM((2 * ROWS, 128), jnp.float32),
            pltpu.VMEM((2 * ROWS, 2 * hs), jnp.float32),
        ],
        compiler_params=pltpu.CompilerParams(vmem_limit_bytes=28 << 20),
        cost_estimate=pl.CostEstimate(
            flops=count * 256 * 4, bytes_accessed=8 << 20, transcendentals=count
        ),
    )(meta, mine, other, shifts, accum, prefix_a, prefix_b)


def split_kernel(queries, keys, values, out):
    for head in range(LOCAL_KV_HEADS):
        out[head, :, q_lanes] = queries[:, 2 * head * hs : 2 * (head + 1) * hs]
        out[head, :, k_lanes] = keys[:, head * hs : (head + 1) * hs]
        out[head, :, v_lanes] = values[:, head * hs : (head + 1) * hs]


def join_kernel(by_head, out):
    for head in range(LOCAL_KV_HEADS):
        out[:, 2 * head * hs : 2 * (head + 1) * hs] = by_head[head]


def relaid(kernel, shape, *operands):
    return pl.pallas_call(
        kernel,
        out_shape=jax.ShapeDtypeStruct(shape, jnp.bfloat16),
        in_specs=[in_vmem] * len(operands),
        out_specs=in_vmem,
        compiler_params=pltpu.CompilerParams(vmem_limit_bytes=12 << 20),
    )(*operands)


def on_device(queries, suffix_keys, suffix_values, prefix_keys, prefix_values, lengths):
    head = lax.axis_index("z")
    second = lax.axis_index("yh").astype(jnp.int32)
    meta = jnp.stack([second, lengths[0]])

    def swapped(array, axis):
        return lax.ppermute(array, axis, [(0, 1), (1, 0)])

    mine = relaid(
        split_kernel,
        (LOCAL_KV_HEADS, ROWS, 4 * hs),
        queries[0],
        suffix_keys[0],
        suffix_values[0],
    )
    mine = lax.all_to_all(mine, "z", 0, 0, tiled=False).reshape(ALL_ROWS, 4 * hs)
    other = swapped(mine[:, 2 * hs :], "yh")

    part = jnp.concatenate(
        [
            lax.dynamic_slice_in_dim(prefix_keys, head * hs, hs, axis=1),
            lax.dynamic_slice_in_dim(prefix_values, head * hs, hs, axis=1),
        ],
        axis=1,
    )
    column = jnp.concatenate(
        [part]
        + [lax.ppermute(part, "x", [(i, (i + shift) % 4) for i in range(4)]) for shift in (1, 3, 2)],
        axis=0,
    )
    prefix_a = jnp.concatenate([column, swapped(column, "yl")], axis=0)
    prefix_b = swapped(prefix_a, "core")

    shifts, accum = prefix_part(mine, prefix_a, prefix_b)
    attended = suffix_part(meta, mine, other, shifts, accum, prefix_a, prefix_b)
    attended = lax.all_to_all(attended.reshape(BLOCKS, ROWS, 2 * hs), "z", 0, 0, tiled=False)
    return relaid(join_kernel, (ROWS, LOCAL_KV_HEADS * 2 * hs), attended)[None]


def solution(mesh):
    fine = Mesh(mesh.devices.reshape(4, 2, 2, 8, 2), ("x", "yl", "core", "z", "yh"))
    grp, seq = ("x", "yl", "core"), ("z", "yh")
    in_specs = (
        P(grp, seq, None),
        P(grp, seq, None),
        P(grp, seq, None),
        P(grp, None),
        P(grp, None),
        P(grp),
    )
    return jax.shard_map(
        on_device, mesh=fine, in_specs=in_specs, out_specs=P(grp, seq, None), check_vma=False
    )
```

```python
import jax
import jax.numpy as jnp
from jax import lax
from jax.experimental import pallas as pl
from jax.experimental.pallas import tpu as pltpu
from jax.sharding import Mesh, PartitionSpec as P

LOCAL_KV_HEADS = 8
HEAD_SIZE = 128
QUERY_PER_KV = 2
ROWS = 192
BLOCKS = 8
ALL_ROWS = BLOCKS * ROWS
PREFIX_HALF = 2048
KEY_TILE = 256

query_scale = 168.0 ** (-0.5)
log2_e = 1.4426950408889634
total_bound = 1e37
hs = HEAD_SIZE
k_lanes = slice(2 * hs, 3 * hs)
v_lanes = slice(3 * hs, 4 * hs)


def scores_of(query_pair, keys):
    return lax.dot_general(
        query_pair,
        jnp.concatenate([keys, keys], axis=1),
        (((1,), (1,)), ((), ())),
        preferred_element_type=jnp.float32,
    )


def weights_of(scores, shift):
    return jnp.exp2(scores - jnp.concatenate([shift] * (scores.shape[1] // 128), axis=1))


def summed_of(weights, values):
    return lax.dot_general(
        weights.astype(jnp.bfloat16),
        jnp.concatenate([values, jnp.ones_like(values)], axis=1),
        (((1,), (0,)), ((), ())),
        preferred_element_type=jnp.float32,
    )


def pair_of(queries):
    scaled = queries.astype(jnp.float32) * (query_scale * log2_e)
    high = scaled.astype(jnp.bfloat16)
    low = (scaled - high.astype(jnp.float32)).astype(jnp.bfloat16)
    return jnp.concatenate([high, low], axis=1)


def prefix_kernel(mine, prefix_a, prefix_b, shifts, accum):
    tiles = [(p, i) for p in (prefix_a, prefix_b) for i in range(0, PREFIX_HALF, KEY_TILE)]

    @pl.loop(0, QUERY_PER_KV)
    def _(member):
        pair = pair_of(mine[:, pl.ds(pl.multiple_of(member * hs, hs), hs)])
        first = scores_of(pair, prefix_a[0:256, 0:hs])
        shift = jnp.broadcast_to(jnp.max(first, axis=1, keepdims=True), (ALL_ROWS, 128))
        scores = scores_of(pair, prefix_a[0:KEY_TILE, 0:hs])
        total = None
        for j, (ref, start) in enumerate(tiles):
            following = None
            if j + 1 < len(tiles):
                next_ref, next_start = tiles[j + 1]
                following = scores_of(pair, next_ref[next_start : next_start + KEY_TILE, 0:hs])
            added = summed_of(weights_of(scores, shift), ref[start : start + KEY_TILE, hs : 2 * hs])
            total = added if total is None else total + added
            scores = following
        shifts[member] = shift
        accum[member] = total


def suffix_kernel(meta, mine, other, shifts, accum, prefix_a, prefix_b, out, peaks, again):
    second = meta[0]
    length = meta[1]
    row_ids = lax.broadcasted_iota(jnp.int32, (2 * ROWS, 2 * ROWS), 0)
    row_ids = jnp.where(row_ids < ROWS, row_ids, row_ids - ROWS)
    col_ids = lax.broadcasted_iota(jnp.int32, (2 * ROWS, 2 * ROWS), 1)
    visible = ((col_ids < ROWS) & (col_ids <= row_ids)) | ((col_ids >= ROWS) & (second == 1))

    def keys_of(block, which):
        parts = []
        if block > 0:
            parts += [mine[0 : block * ROWS, (k_lanes, v_lanes)[which]]]
            parts += [other[0 : block * ROWS, which * hs : (which + 1) * hs]]
        rows = slice(block * ROWS, (block + 1) * ROWS)
        parts += [mine[rows, (k_lanes, v_lanes)[which]]]
        parts += [other[rows, which * hs : (which + 1) * hs]]
        return jnp.concatenate(parts, axis=0)

    def both(ref, block):
        return jnp.concatenate([ref[m, block * ROWS : (block + 1) * ROWS, :] for m in range(2)], axis=0)

    def members_of(rows):
        return jnp.concatenate([mine[rows, 0:hs], mine[rows, hs : 2 * hs]], axis=0)

    def suffix_scores(block):
        queries = members_of(slice(block * ROWS, (block + 1) * ROWS))
        return scores_of(pair_of(queries), keys_of(block, 0))

    def finish(block, total):
        result = total[:, 0:hs] / total[:, hs : 2 * hs]
        result = jnp.concatenate([result[0:ROWS], result[ROWS : 2 * ROWS]], axis=1)
        row = lax.broadcasted_iota(jnp.int32, (ROWS, 2 * hs), 0)
        live = (2 * block + second) * ROWS + row < length
        return jnp.where(live, result, 0.0).astype(jnp.bfloat16)

    scores = suffix_scores(0)
    beyond = jnp.zeros((2 * ROWS, hs), jnp.float32)
    for block in range(BLOCKS):
        following = suffix_scores(block + 1) if block + 1 < BLOCKS else None
        weights = weights_of(scores, both(shifts, block))
        edge = 2 * ROWS * block
        masked = jnp.where(visible, weights[:, edge:], 0.0)
        weights = jnp.concatenate([weights[:, :edge], masked], axis=1) if block > 0 else masked
        total = both(accum, block) + summed_of(weights, keys_of(block, 1))
        beyond = jnp.maximum(beyond, jnp.where(total[:, hs:] < total_bound, 0.0, 1.0))
        out[block * ROWS : (block + 1) * ROWS, :] = finish(block, total)
        scores = following

    @pl.when(jnp.max(beyond) > 0.0)
    def _():
        @pl.loop(0, BLOCKS)
        def _(block):
            rows = pl.ds(pl.multiple_of(block * ROWS, ROWS), ROWS)
            pair = pair_of(members_of(rows))
            peaks[...] = jnp.full((2 * ROWS, 128), -1e30, jnp.float32)
            again[...] = jnp.zeros((2 * ROWS, 2 * hs), jnp.float32)

            def step(keys, values, seen):
                part = scores_of(pair, keys)
                if seen is not None:
                    part = jnp.where(seen, part, -1e30)
                old = peaks[:, 0:1]
                new = jnp.maximum(old, jnp.max(part, axis=1, keepdims=True))
                weights = jnp.exp2(part - new)
                again[...] = again[...] * jnp.exp2(old - new) + summed_of(weights, values)
                peaks[...] = jnp.broadcast_to(new, (2 * ROWS, 128))

            for ref in (prefix_a, prefix_b):

                @pl.loop(0, PREFIX_HALF // 256)
                def _(i):
                    keys = pl.ds(pl.multiple_of(i * 256, 256), 256)
                    step(ref[keys, 0:hs], ref[keys, hs : 2 * hs], None)

            row = lax.broadcasted_iota(jnp.int32, (2 * ROWS, ROWS), 0)
            row = jnp.where(row < ROWS, row, row - ROWS)
            col = lax.broadcasted_iota(jnp.int32, (2 * ROWS, ROWS), 1)

            @pl.loop(0, block + 1)
            def _(i):
                keys = pl.ds(pl.multiple_of(i * ROWS, ROWS), ROWS)
                step(mine[keys, k_lanes], mine[keys, v_lanes], (col <= row) | (i < block))
                full = (i < block) | (second == 1)
                step(other[keys, 0:hs], other[keys, hs : 2 * hs], (col >= 0) & full)

            out[rows, :] = finish(block, again[...])


in_vmem = pl.BlockSpec(memory_space=pltpu.VMEM)


def call(kernel, shapes, operands, scratch=(), scores=0, limit=24, specs=None):
    return pl.pallas_call(
        kernel,
        out_shape=shapes,
        in_specs=specs or [in_vmem] * len(operands),
        out_specs=jax.tree.map(lambda _: in_vmem, shapes),
        scratch_shapes=scratch,
        compiler_params=pltpu.CompilerParams(vmem_limit_bytes=limit << 20),
        cost_estimate=pl.CostEstimate(
            flops=scores * 256 * 4, bytes_accessed=4 << 20, transcendentals=scores
        ),
    )(*operands)


def f32(*shape):
    return jax.ShapeDtypeStruct(shape, jnp.float32)


def bf16(*shape):
    return jax.ShapeDtypeStruct(shape, jnp.bfloat16)


in_smem = pl.BlockSpec(memory_space=pltpu.SMEM)
in_place = pl.BlockSpec(memory_space=pl.ANY)


def split_kernel(queries, keys, values, out, sem):
    copies = []

    def copy(source, target):
        copies.append(pltpu.make_async_copy(source, target, sem.at[len(copies)]))
        copies[-1].start()

    for head in range(LOCAL_KV_HEADS):
        lanes = pl.ds(head * hs, hs)
        copy(queries.at[:, pl.ds(2 * head * hs, 2 * hs)], out.at[head, :, pl.ds(0, 2 * hs)])
        copy(keys.at[:, lanes], out.at[head, :, k_lanes])
        copy(values.at[:, lanes], out.at[head, :, v_lanes])
    for one in copies:
        one.wait()


def join_kernel(by_head, out):
    for head in range(LOCAL_KV_HEADS):
        out[:, 2 * head * hs : 2 * (head + 1) * hs] = by_head[head]


def on_device(queries, suffix_keys, suffix_values, prefix_keys, prefix_values, lengths):
    head = lax.axis_index("z")
    second = lax.axis_index("yh").astype(jnp.int32)
    meta = jnp.stack([second, lengths[0]])

    def swapped(array, axis):
        return lax.ppermute(array, axis, [(0, 1), (1, 0)])

    mine = call(
        split_kernel,
        bf16(LOCAL_KV_HEADS, ROWS, 4 * hs),
        (queries[0], suffix_keys[0], suffix_values[0]),
        scratch=[pltpu.SemaphoreType.DMA((3 * LOCAL_KV_HEADS,))],
        limit=60,
        specs=[in_place] * 3,
    )
    mine = lax.all_to_all(mine, "z", 0, 0, tiled=False).reshape(ALL_ROWS, 4 * hs)
    other = swapped(mine[:, 2 * hs :], "yh")

    part = jnp.concatenate(
        [
            lax.dynamic_slice_in_dim(prefix_keys, head * hs, hs, axis=1),
            lax.dynamic_slice_in_dim(prefix_values, head * hs, hs, axis=1),
        ],
        axis=1,
    )
    column = jnp.concatenate(
        [part]
        + [lax.ppermute(part, "x", [(i, (i + shift) % 4) for i in range(4)]) for shift in (1, 3, 2)],
        axis=0,
    )
    prefix_a = jnp.concatenate([column, swapped(column, "yl")], axis=0)
    prefix_b = swapped(prefix_a, "core")

    state = call(
        prefix_kernel,
        (f32(2, ALL_ROWS, 128), f32(2, ALL_ROWS, 2 * hs)),
        (mine, prefix_a, prefix_b),
        scores=4 * ALL_ROWS * PREFIX_HALF,
    )
    attended = call(
        suffix_kernel,
        bf16(ALL_ROWS, 2 * hs),
        (meta, mine, other, *state, prefix_a, prefix_b),
        scratch=[pltpu.VMEM((2 * ROWS, 128), jnp.float32), pltpu.VMEM((2 * ROWS, 2 * hs), jnp.float32)],
        scores=2 * ALL_ROWS * ALL_ROWS,
        limit=28,
        specs=[in_smem] + [in_vmem] * 6,
    )
    attended = lax.all_to_all(attended.reshape(BLOCKS, ROWS, 2 * hs), "z", 0, 0, tiled=False)
    return call(join_kernel, bf16(ROWS, LOCAL_KV_HEADS * 2 * hs), (attended,), limit=12)[None]


def solution(mesh):
    fine = Mesh(mesh.devices.reshape(4, 2, 2, 8, 2), ("x", "yl", "core", "z", "yh"))
    grp, seq = ("x", "yl", "core"), ("z", "yh")
    in_specs = (
        P(grp, seq, None),
        P(grp, seq, None),
        P(grp, seq, None),
        P(grp, None),
        P(grp, None),
        P(grp),
    )
    return jax.shard_map(
        on_device, mesh=fine, in_specs=in_specs, out_specs=P(grp, seq, None), check_vma=False
    )
```

```python
import jax
import jax.numpy as jnp
from jax import lax
from jax.experimental import pallas as pl
from jax.experimental.pallas import tpu as pltpu
from jax.sharding import Mesh, PartitionSpec as P

LOCAL_KV_HEADS = 8
HEAD_SIZE = 128
QUERY_PER_KV = 2
ROWS = 192
BLOCKS = 8
ALL_ROWS = BLOCKS * ROWS
PREFIX_HALF = 2048
KEY_TILE = 256

query_scale = 168.0 ** (-0.5)
log2_e = 1.4426950408889634
total_bound = 1e37
hs = HEAD_SIZE
k_lanes = slice(2 * hs, 3 * hs)
v_lanes = slice(3 * hs, 4 * hs)


def scores_of(query_pair, keys):
    return lax.dot_general(
        query_pair,
        jnp.concatenate([keys, keys], axis=1),
        (((1,), (1,)), ((), ())),
        preferred_element_type=jnp.float32,
    )


def weights_of(scores, shift):
    return jnp.exp2(scores - jnp.concatenate([shift] * (scores.shape[1] // 128), axis=1))


def summed_of(weights, values):
    return lax.dot_general(
        weights.astype(jnp.bfloat16),
        jnp.concatenate([values, jnp.ones_like(values)], axis=1),
        (((1,), (0,)), ((), ())),
        preferred_element_type=jnp.float32,
    )


def pair_of(queries):
    scaled = queries.astype(jnp.float32) * (query_scale * log2_e)
    high = scaled.astype(jnp.bfloat16)
    low = (scaled - high.astype(jnp.float32)).astype(jnp.bfloat16)
    return jnp.concatenate([high, low], axis=1)


def prefix_kernel(mine, prefix_a, prefix_b, shifts, accum):
    tiles = [(p, i) for p in (prefix_a, prefix_b) for i in range(0, PREFIX_HALF, KEY_TILE)]

    @pl.loop(0, QUERY_PER_KV)
    def _(member):
        pair = pair_of(mine[:, pl.ds(pl.multiple_of(member * hs, hs), hs)])
        first = scores_of(pair, prefix_a[0:256, 0:hs])
        shift = jnp.broadcast_to(jnp.max(first, axis=1, keepdims=True), (ALL_ROWS, 128))
        shifts[member] = shift
        scores = scores_of(pair, prefix_a[0:KEY_TILE, 0:hs])
        for j, (ref, start) in enumerate(tiles):
            following = None
            if j + 1 < len(tiles):
                next_ref, next_start = tiles[j + 1]
                following = scores_of(pair, next_ref[next_start : next_start + KEY_TILE, 0:hs])
            added = summed_of(weights_of(scores, shift), ref[start : start + KEY_TILE, hs : 2 * hs])
            accum[member] = added if j == 0 else accum[member] + added
            scores = following


def suffix_kernel(meta, mine, other, shifts, accum, prefix_a, prefix_b, out, peaks, again, held):
    second = meta[0]
    length = meta[1]
    row_ids = lax.broadcasted_iota(jnp.int32, (2 * ROWS, 2 * ROWS), 0)
    row_ids = jnp.where(row_ids < ROWS, row_ids, row_ids - ROWS)
    col_ids = lax.broadcasted_iota(jnp.int32, (2 * ROWS, 2 * ROWS), 1)
    visible = ((col_ids < ROWS) & (col_ids <= row_ids)) | ((col_ids >= ROWS) & (second == 1))

    def keys_of(block, which):
        parts = []
        if block > 0:
            parts += [mine[0 : block * ROWS, (k_lanes, v_lanes)[which]]]
            parts += [other[0 : block * ROWS, which * hs : (which + 1) * hs]]
        rows = slice(block * ROWS, (block + 1) * ROWS)
        parts += [mine[rows, (k_lanes, v_lanes)[which]]]
        parts += [other[rows, which * hs : (which + 1) * hs]]
        return jnp.concatenate(parts, axis=0)

    def both(ref, block):
        return jnp.concatenate([ref[m, block * ROWS : (block + 1) * ROWS, :] for m in range(2)], axis=0)

    def members_of(rows):
        return jnp.concatenate([mine[rows, 0:hs], mine[rows, hs : 2 * hs]], axis=0)

    def suffix_scores(block):
        queries = members_of(slice(block * ROWS, (block + 1) * ROWS))
        return scores_of(pair_of(queries), keys_of(block, 0))

    def finish(block, total):
        result = total[:, 0:hs] / total[:, hs : 2 * hs]
        result = jnp.concatenate([result[0:ROWS], result[ROWS : 2 * ROWS]], axis=1)
        row = lax.broadcasted_iota(jnp.int32, (ROWS, 2 * hs), 0)
        live = (2 * block + second) * ROWS + row < length
        return jnp.where(live, result, 0.0).astype(jnp.bfloat16)

    scores = suffix_scores(0)
    beyond = jnp.zeros((2 * ROWS, hs), jnp.float32)
    for block in range(BLOCKS):
        following = suffix_scores(block + 1) if block + 1 < BLOCKS else None
        weights = weights_of(scores, both(shifts, block))
        edge = 2 * ROWS * block
        masked = jnp.where(visible, weights[:, edge:], 0.0)
        weights = jnp.concatenate([weights[:, :edge], masked], axis=1) if block > 0 else masked
        total = both(accum, block) + summed_of(weights, keys_of(block, 1))
        beyond = jnp.maximum(beyond, jnp.where(total[:, hs:] < total_bound, 0.0, 1.0))
        out[block * ROWS : (block + 1) * ROWS, :] = finish(block, total)
        scores = following

    @pl.when(jnp.max(beyond) > 0.0)
    def _():
        pltpu.sync_copy(prefix_b, held)

        @pl.loop(0, BLOCKS)
        def _(block):
            rows = pl.ds(pl.multiple_of(block * ROWS, ROWS), ROWS)
            pair = pair_of(members_of(rows))
            peaks[...] = jnp.full((2 * ROWS, 128), -1e30, jnp.float32)
            again[...] = jnp.zeros((2 * ROWS, 2 * hs), jnp.float32)

            def step(keys, values, seen):
                part = scores_of(pair, keys)
                if seen is not None:
                    part = jnp.where(seen, part, -1e30)
                old = peaks[:, 0:1]
                new = jnp.maximum(old, jnp.max(part, axis=1, keepdims=True))
                weights = jnp.exp2(part - new)
                again[...] = again[...] * jnp.exp2(old - new) + summed_of(weights, values)
                peaks[...] = jnp.broadcast_to(new, (2 * ROWS, 128))

            for ref in (prefix_a, held):

                @pl.loop(0, PREFIX_HALF // 256)
                def _(i):
                    keys = pl.ds(pl.multiple_of(i * 256, 256), 256)
                    step(ref[keys, 0:hs], ref[keys, hs : 2 * hs], None)

            row = lax.broadcasted_iota(jnp.int32, (2 * ROWS, ROWS), 0)
            row = jnp.where(row < ROWS, row, row - ROWS)
            col = lax.broadcasted_iota(jnp.int32, (2 * ROWS, ROWS), 1)

            @pl.loop(0, block + 1)
            def _(i):
                keys = pl.ds(pl.multiple_of(i * ROWS, ROWS), ROWS)
                step(mine[keys, k_lanes], mine[keys, v_lanes], (col <= row) | (i < block))
                full = (i < block) | (second == 1)
                step(other[keys, 0:hs], other[keys, hs : 2 * hs], (col >= 0) & full)

            out[rows, :] = finish(block, again[...])


in_vmem = pl.BlockSpec(memory_space=pltpu.VMEM)


def call(kernel, shapes, operands, scratch=(), scores=0, limit=24, specs=None, outs=None):
    return pl.pallas_call(
        kernel,
        out_shape=shapes,
        in_specs=specs or [in_vmem] * len(operands),
        out_specs=outs or jax.tree.map(lambda _: in_vmem, shapes),
        scratch_shapes=scratch,
        compiler_params=pltpu.CompilerParams(vmem_limit_bytes=limit << 20),
        cost_estimate=pl.CostEstimate(
            flops=scores * 256 * 4, bytes_accessed=4 << 20, transcendentals=scores
        ),
    )(*operands)


def f32(*shape):
    return jax.ShapeDtypeStruct(shape, jnp.float32)


def bf16(*shape):
    return jax.ShapeDtypeStruct(shape, jnp.bfloat16)


in_smem = pl.BlockSpec(memory_space=pltpu.SMEM)
in_place = pl.BlockSpec(memory_space=pl.ANY)


def split_kernel(queries, keys, values, out, held, arrived, left):
    arriving, leaving = [], []
    for head in range(LOCAL_KV_HEADS):
        lanes = pl.ds(head * hs, hs)
        parts = (
            (queries.at[:, pl.ds(2 * head * hs, 2 * hs)], pl.ds(0, 2 * hs)),
            (keys.at[:, lanes], pl.ds(2 * hs, hs)),
            (values.at[:, lanes], pl.ds(3 * hs, hs)),
        )
        arriving.append(
            [
                pltpu.make_async_copy(source, held.at[head, :, target], arrived.at[head, i])
                for i, (source, target) in enumerate(parts)
            ]
        )
        for copy in arriving[-1]:
            copy.start()
    for head in range(LOCAL_KV_HEADS):
        for copy in arriving[head]:
            copy.wait()
        leaving.append(pltpu.make_async_copy(held.at[head], out.at[head], left.at[head]))
        leaving[-1].start()
    for copy in leaving:
        copy.wait()


def join_kernel(by_head, out):
    for head in range(LOCAL_KV_HEADS):
        out[:, 2 * head * hs : 2 * (head + 1) * hs] = by_head[head]


def on_device(queries, suffix_keys, suffix_values, prefix_keys, prefix_values, lengths):
    head = lax.axis_index("z")
    second = lax.axis_index("yh").astype(jnp.int32)
    meta = jnp.stack([second, lengths[0]])

    def swapped(array, axis):
        return lax.ppermute(array, axis, [(0, 1), (1, 0)])

    mine = call(
        split_kernel,
        bf16(LOCAL_KV_HEADS, ROWS, 4 * hs),
        (queries[0], suffix_keys[0], suffix_values[0]),
        scratch=[
            pltpu.VMEM((LOCAL_KV_HEADS, ROWS, 4 * hs), jnp.bfloat16),
            pltpu.SemaphoreType.DMA((LOCAL_KV_HEADS, 3)),
            pltpu.SemaphoreType.DMA((LOCAL_KV_HEADS,)),
        ],
        limit=60,
        specs=[in_place] * 3,
        outs=in_place,
    )
    mine = lax.all_to_all(mine, "z", 0, 0, tiled=False).reshape(ALL_ROWS, 4 * hs)
    other = swapped(mine[:, 2 * hs :], "yh")

    part = jnp.concatenate(
        [
            lax.dynamic_slice_in_dim(prefix_keys, head * hs, hs, axis=1),
            lax.dynamic_slice_in_dim(prefix_values, head * hs, hs, axis=1),
        ],
        axis=1,
    )
    column = jnp.concatenate(
        [part]
        + [lax.ppermute(part, "x", [(i, (i + shift) % 4) for i in range(4)]) for shift in (1, 3, 2)],
        axis=0,
    )
    prefix_a = jnp.concatenate([column, swapped(column, "yl")], axis=0)
    prefix_b = swapped(prefix_a, "core")

    state = call(
        prefix_kernel,
        (f32(2, ALL_ROWS, 128), f32(2, ALL_ROWS, 2 * hs)),
        (mine, prefix_a, prefix_b),
        scores=4 * ALL_ROWS * PREFIX_HALF,
    )
    attended = call(
        suffix_kernel,
        bf16(ALL_ROWS, 2 * hs),
        (meta, mine, other, *state, prefix_a, prefix_b),
        scratch=[pltpu.VMEM((2 * ROWS, 128), jnp.float32), pltpu.VMEM((2 * ROWS, 2 * hs), jnp.float32), pltpu.VMEM((PREFIX_HALF, 2 * hs), jnp.bfloat16)],
        scores=2 * ALL_ROWS * ALL_ROWS,
        limit=28,
        specs=[in_smem] + [in_vmem] * 5 + [in_place],
    )
    attended = lax.all_to_all(attended.reshape(BLOCKS, ROWS, 2 * hs), "z", 0, 0, tiled=False)
    return call(join_kernel, bf16(ROWS, LOCAL_KV_HEADS * 2 * hs), (attended,), limit=12)[None]


def solution(mesh):
    fine = Mesh(mesh.devices.reshape(4, 2, 2, 8, 2), ("x", "yl", "core", "z", "yh"))
    grp, seq = ("x", "yl", "core"), ("z", "yh")
    in_specs = (
        P(grp, seq, None),
        P(grp, seq, None),
        P(grp, seq, None),
        P(grp, None),
        P(grp, None),
        P(grp),
    )
    return jax.shard_map(
        on_device, mesh=fine, in_specs=in_specs, out_specs=P(grp, seq, None), check_vma=False
    )
```

```python
import jax
import jax.numpy as jnp
from jax import lax
from jax.experimental import pallas as pl
from jax.experimental.pallas import tpu as pltpu
from jax.sharding import Mesh, PartitionSpec as P

LOCAL_KV_HEADS = 8
HEAD_SIZE = 128
QUERY_PER_KV = 2
ROWS = 192
BLOCKS = 8
ALL_ROWS = BLOCKS * ROWS
PREFIX_HALF = 2048
KEY_TILE = 256

query_scale = 168.0 ** (-0.5)
log2_e = 1.4426950408889634
total_bound = 1e37
hs = HEAD_SIZE
k_lanes = slice(2 * hs, 3 * hs)
v_lanes = slice(3 * hs, 4 * hs)


def scores_of(query_pair, keys):
    return lax.dot_general(
        query_pair,
        jnp.concatenate([keys, keys], axis=1),
        (((1,), (1,)), ((), ())),
        preferred_element_type=jnp.float32,
    )


def weights_of(scores, shift):
    return jnp.exp2(scores - jnp.concatenate([shift] * (scores.shape[1] // 128), axis=1))


def summed_of(weights, values):
    return lax.dot_general(
        weights.astype(jnp.bfloat16),
        jnp.concatenate([values, jnp.ones_like(values)], axis=1),
        (((1,), (0,)), ((), ())),
        preferred_element_type=jnp.float32,
    )


def pair_of(queries):
    scaled = queries.astype(jnp.float32) * (query_scale * log2_e)
    high = scaled.astype(jnp.bfloat16)
    low = (scaled - high.astype(jnp.float32)).astype(jnp.bfloat16)
    return jnp.concatenate([high, low], axis=1)


def prefix_kernel(mine, prefix_a, prefix_b, shifts, accum, held, arrived):
    arriving = pltpu.make_async_copy(prefix_b, held, arrived)
    arriving.start()
    tiles = [(p, i) for p in (prefix_a, held) for i in range(0, PREFIX_HALF, KEY_TILE)]

    @pl.loop(0, QUERY_PER_KV)
    def _(member):
        pair = pair_of(mine[:, pl.ds(pl.multiple_of(member * hs, hs), hs)])
        first = scores_of(pair, prefix_a[0:256, 0:hs])
        shift = jnp.broadcast_to(jnp.max(first, axis=1, keepdims=True), (ALL_ROWS, 128))
        shifts[member] = shift
        pl.when(member == 0)(arriving.wait)
        scores = scores_of(pair, prefix_a[0:KEY_TILE, 0:hs])
        for j, (ref, start) in enumerate(tiles):
            following = None
            if j + 1 < len(tiles):
                next_ref, next_start = tiles[j + 1]
                following = scores_of(pair, next_ref[next_start : next_start + KEY_TILE, 0:hs])
            added = summed_of(weights_of(scores, shift), ref[start : start + KEY_TILE, hs : 2 * hs])
            accum[member] = added if j == 0 else accum[member] + added
            scores = following


def suffix_kernel(meta, mine, other, shifts, accum, prefix_a, prefix_b, out, peaks, again, held):
    second = meta[0]
    length = meta[1]
    row_ids = lax.broadcasted_iota(jnp.int32, (2 * ROWS, 2 * ROWS), 0)
    row_ids = jnp.where(row_ids < ROWS, row_ids, row_ids - ROWS)
    col_ids = lax.broadcasted_iota(jnp.int32, (2 * ROWS, 2 * ROWS), 1)
    visible = ((col_ids < ROWS) & (col_ids <= row_ids)) | ((col_ids >= ROWS) & (second == 1))

    def keys_of(block, which):
        parts = []
        if block > 0:
            parts += [mine[0 : block * ROWS, (k_lanes, v_lanes)[which]]]
            parts += [other[0 : block * ROWS, which * hs : (which + 1) * hs]]
        rows = slice(block * ROWS, (block + 1) * ROWS)
        parts += [mine[rows, (k_lanes, v_lanes)[which]]]
        parts += [other[rows, which * hs : (which + 1) * hs]]
        return jnp.concatenate(parts, axis=0)

    def both(ref, block):
        return jnp.concatenate([ref[m, block * ROWS : (block + 1) * ROWS, :] for m in range(2)], axis=0)

    def members_of(rows):
        return jnp.concatenate([mine[rows, 0:hs], mine[rows, hs : 2 * hs]], axis=0)

    def suffix_scores(block):
        queries = members_of(slice(block * ROWS, (block + 1) * ROWS))
        return scores_of(pair_of(queries), keys_of(block, 0))

    def finish(block, total):
        result = total[:, 0:hs] / total[:, hs : 2 * hs]
        result = jnp.concatenate([result[0:ROWS], result[ROWS : 2 * ROWS]], axis=1)
        row = lax.broadcasted_iota(jnp.int32, (ROWS, 2 * hs), 0)
        live = (2 * block + second) * ROWS + row < length
        return jnp.where(live, result, 0.0).astype(jnp.bfloat16)

    scores = suffix_scores(0)
    beyond = jnp.zeros((2 * ROWS, hs), jnp.float32)
    for block in range(BLOCKS):
        following = suffix_scores(block + 1) if block + 1 < BLOCKS else None
        weights = weights_of(scores, both(shifts, block))
        edge = 2 * ROWS * block
        masked = jnp.where(visible, weights[:, edge:], 0.0)
        weights = jnp.concatenate([weights[:, :edge], masked], axis=1) if block > 0 else masked
        total = both(accum, block) + summed_of(weights, keys_of(block, 1))
        beyond = jnp.maximum(beyond, jnp.where(total[:, hs:] < total_bound, 0.0, 1.0))
        out[block * ROWS : (block + 1) * ROWS, :] = finish(block, total)
        scores = following

    @pl.when(jnp.max(beyond) > 0.0)
    def _():
        pltpu.sync_copy(prefix_b, held)

        @pl.loop(0, BLOCKS)
        def _(block):
            rows = pl.ds(pl.multiple_of(block * ROWS, ROWS), ROWS)
            pair = pair_of(members_of(rows))
            peaks[...] = jnp.full((2 * ROWS, 128), -1e30, jnp.float32)
            again[...] = jnp.zeros((2 * ROWS, 2 * hs), jnp.float32)

            def step(keys, values, seen):
                part = scores_of(pair, keys)
                if seen is not None:
                    part = jnp.where(seen, part, -1e30)
                old = peaks[:, 0:1]
                new = jnp.maximum(old, jnp.max(part, axis=1, keepdims=True))
                weights = jnp.exp2(part - new)
                again[...] = again[...] * jnp.exp2(old - new) + summed_of(weights, values)
                peaks[...] = jnp.broadcast_to(new, (2 * ROWS, 128))

            for ref in (prefix_a, held):

                @pl.loop(0, PREFIX_HALF // 256)
                def _(i):
                    keys = pl.ds(pl.multiple_of(i * 256, 256), 256)
                    step(ref[keys, 0:hs], ref[keys, hs : 2 * hs], None)

            row = lax.broadcasted_iota(jnp.int32, (2 * ROWS, ROWS), 0)
            row = jnp.where(row < ROWS, row, row - ROWS)
            col = lax.broadcasted_iota(jnp.int32, (2 * ROWS, ROWS), 1)

            @pl.loop(0, block + 1)
            def _(i):
                keys = pl.ds(pl.multiple_of(i * ROWS, ROWS), ROWS)
                step(mine[keys, k_lanes], mine[keys, v_lanes], (col <= row) | (i < block))
                full = (i < block) | (second == 1)
                step(other[keys, 0:hs], other[keys, hs : 2 * hs], (col >= 0) & full)

            out[rows, :] = finish(block, again[...])


in_vmem = pl.BlockSpec(memory_space=pltpu.VMEM)


def call(kernel, shapes, operands, scratch=(), scores=0, limit=24, specs=None, outs=None):
    return pl.pallas_call(
        kernel,
        out_shape=shapes,
        in_specs=specs or [in_vmem] * len(operands),
        out_specs=outs or jax.tree.map(lambda _: in_vmem, shapes),
        scratch_shapes=scratch,
        compiler_params=pltpu.CompilerParams(vmem_limit_bytes=limit << 20),
        cost_estimate=pl.CostEstimate(
            flops=scores * 256 * 4, bytes_accessed=4 << 20, transcendentals=scores
        ),
    )(*operands)


def f32(*shape):
    return jax.ShapeDtypeStruct(shape, jnp.float32)


def bf16(*shape):
    return jax.ShapeDtypeStruct(shape, jnp.bfloat16)


in_smem = pl.BlockSpec(memory_space=pltpu.SMEM)
in_place = pl.BlockSpec(memory_space=pl.ANY)


def split_kernel(queries, keys, values, out, held, arrived, left):
    arriving, leaving = [], []
    for head in range(LOCAL_KV_HEADS):
        lanes = pl.ds(head * hs, hs)
        parts = (
            (queries.at[:, pl.ds(2 * head * hs, 2 * hs)], pl.ds(0, 2 * hs)),
            (keys.at[:, lanes], pl.ds(2 * hs, hs)),
            (values.at[:, lanes], pl.ds(3 * hs, hs)),
        )
        arriving.append(
            [
                pltpu.make_async_copy(source, held.at[head, :, target], arrived.at[head, i])
                for i, (source, target) in enumerate(parts)
            ]
        )
        for copy in arriving[-1]:
            copy.start()
    for head in range(LOCAL_KV_HEADS):
        for copy in arriving[head]:
            copy.wait()
        leaving.append(pltpu.make_async_copy(held.at[head], out.at[head], left.at[head]))
        leaving[-1].start()
    for copy in leaving:
        copy.wait()


def join_kernel(by_head, out):
    for head in range(LOCAL_KV_HEADS):
        out[:, 2 * head * hs : 2 * (head + 1) * hs] = by_head[head]


def on_device(queries, suffix_keys, suffix_values, prefix_keys, prefix_values, lengths):
    head = lax.axis_index("z")
    second = lax.axis_index("yh").astype(jnp.int32)
    meta = jnp.stack([second, lengths[0]])

    def swapped(array, axis):
        return lax.ppermute(array, axis, [(0, 1), (1, 0)])

    mine = call(
        split_kernel,
        bf16(LOCAL_KV_HEADS, ROWS, 4 * hs),
        (queries[0], suffix_keys[0], suffix_values[0]),
        scratch=[
            pltpu.VMEM((LOCAL_KV_HEADS, ROWS, 4 * hs), jnp.bfloat16),
            pltpu.SemaphoreType.DMA((LOCAL_KV_HEADS, 3)),
            pltpu.SemaphoreType.DMA((LOCAL_KV_HEADS,)),
        ],
        limit=60,
        specs=[in_place] * 3,
        outs=in_place,
    )
    mine = lax.all_to_all(mine, "z", 0, 0, tiled=False).reshape(ALL_ROWS, 4 * hs)
    other = swapped(mine[:, 2 * hs :], "yh")

    part = jnp.concatenate(
        [
            lax.dynamic_slice_in_dim(prefix_keys, head * hs, hs, axis=1),
            lax.dynamic_slice_in_dim(prefix_values, head * hs, hs, axis=1),
        ],
        axis=1,
    )
    column = jnp.concatenate(
        [part]
        + [lax.ppermute(part, "x", [(i, (i + shift) % 4) for i in range(4)]) for shift in (1, 3, 2)],
        axis=0,
    )
    prefix_a = jnp.concatenate([column, swapped(column, "yl")], axis=0)
    prefix_b = swapped(prefix_a, "core")

    state = call(
        prefix_kernel,
        (f32(2, ALL_ROWS, 128), f32(2, ALL_ROWS, 2 * hs)),
        (mine, prefix_a, prefix_b),
        scratch=[pltpu.VMEM((PREFIX_HALF, 2 * hs), jnp.bfloat16), pltpu.SemaphoreType.DMA],
        specs=[in_vmem] * 2 + [in_place],
        scores=4 * ALL_ROWS * PREFIX_HALF,
    )
    attended = call(
        suffix_kernel,
        bf16(ALL_ROWS, 2 * hs),
        (meta, mine, other, *state, prefix_a, prefix_b),
        scratch=[pltpu.VMEM((2 * ROWS, 128), jnp.float32), pltpu.VMEM((2 * ROWS, 2 * hs), jnp.float32), pltpu.VMEM((PREFIX_HALF, 2 * hs), jnp.bfloat16)],
        scores=2 * ALL_ROWS * ALL_ROWS,
        limit=28,
        specs=[in_smem] + [in_vmem] * 5 + [in_place],
    )
    attended = lax.all_to_all(attended.reshape(BLOCKS, ROWS, 2 * hs), "z", 0, 0, tiled=False)
    return call(join_kernel, bf16(ROWS, LOCAL_KV_HEADS * 2 * hs), (attended,), limit=12)[None]


def solution(mesh):
    fine = Mesh(mesh.devices.reshape(4, 2, 2, 8, 2), ("x", "yl", "core", "z", "yh"))
    grp, seq = ("x", "yl", "core"), ("z", "yh")
    in_specs = (
        P(grp, seq, None),
        P(grp, seq, None),
        P(grp, seq, None),
        P(grp, None),
        P(grp, None),
        P(grp),
    )
    return jax.shard_map(
        on_device, mesh=fine, in_specs=in_specs, out_specs=P(grp, seq, None), check_vma=False
    )
```
